256 devices in a mesh: cp: 128 (over y, x_lo, z, core), kv: 2 (over x_hi).
Axes of the slice: x: 4 (x_hi: 2, x_lo: 2; x = x_hi * 2 + x_lo), y: 4, z: 8, core: 2. Of those that a mesh axis runs over, the one named last changes fastest.
Arguments:
- queries: bfloat16 [32768, 4096], P('cp', 'kv'), may hold values from -48 to 48, as said below
- keys: bfloat16 [32768, 1024], P('cp'), may hold values from -8 to 8, as said below
- values: bfloat16 [32768, 1024], P('cp'), may hold values from -6 to 6
- out_grad: bfloat16 [32768, 4096], P('cp', 'kv'), may hold values from -6 to 6
- block_position: int32 [128], replicated, may hold values from 0 to 127, each once
Outputs:
- attended: bfloat16 [32768, 4096], P('cp', 'kv')
- query_grad: bfloat16 [32768, 4096], P('cp', 'kv')
- key_grad: bfloat16 [32768, 1024], P('cp', 'kv')
- value_grad: bfloat16 [32768, 1024], P('cp', 'kv')
The draws below stay inside these ranges and needn't reach their ends.
Inputs may be any that keep to these rules, and one draw needn't show every extreme that they name: `queries`: real values. `keys`: real values.
All inputs are finite; a program needn't handle non-finite values.
Results may differ from the reference program's by a relative error of at most 0.023.
Values may be sent and summed in bfloat16 or wider, within the bound.
No kernel may reach another device: no remote copies, remote signals or barrier semaphores. Data moves between devices by JAX's collectives and lax.ppermute only.
A program may use at most 128 MiB of HBM per device.

```python
import jax
import jax.numpy as jnp
from jax import lax

QH = 32
KVH = 8
HD = 128
BLK = 256
ROUNDS = 2
BLOCKS = 128
TOKENS = 32768


def draw_queries(key, part):
    key = jax.random.fold_in(key, 1)
    drawn = 2.0 * jnp.clip(jax.random.normal(key, (TOKENS, QH, HD), jnp.float32), -6.0, 6.0)
    return drawn.reshape(TOKENS, QH * HD).astype(jnp.bfloat16)


def draw_keys(key, part):
    key = jax.random.fold_in(key, 2)
    drawn = jnp.clip(jax.random.normal(key, (TOKENS, KVH, HD), jnp.float32), -6.0, 6.0)
    return drawn.reshape(TOKENS, KVH * HD).astype(jnp.bfloat16)


def steps_of(stream_key, dims, pieces, smallest, top_value):
    factor_of = 1.0
    for dim, parts in pieces:
        heights = jax.random.uniform(jax.random.fold_in(jax.random.fold_in(stream_key, 6), dim), (parts,), jnp.float32, smallest / len(pieces), top_value / len(pieces))
        factor_of = factor_of * jnp.repeat(jnp.exp(heights), dims[dim] // parts).reshape((-1,) + (1,) * (len(dims) - 1 - dim))
    return factor_of


def noise(own_key, dims, spread, most, split=(), held_as=jnp.bfloat16):
    factor_of = steps_of(own_key, dims, split, -0.22, 0.18) if split else 1.0
    result = jax.random.normal(own_key, dims, jnp.float32) * spread * factor_of
    return jnp.minimum(jnp.maximum(result, -most), most).astype(held_as)


def setup_inputs(seed: int = 0) -> dict:
    streams_of = jax.random.split(jax.random.key(seed), 6)
    queries = draw_queries(jax.random.fold_in(streams_of[5], 71), 0)
    keys = draw_keys(jax.random.fold_in(streams_of[5], 71), 0)
    values = noise(streams_of[2], (TOKENS, KVH * HD), 1.0, 6.0, ((0, 128),))
    out_grad = noise(streams_of[3], (TOKENS, QH * HD), 1.0, 6.0, ((0, 128), (1, 2)))
    block_position = jax.random.permutation(streams_of[4], BLOCKS).astype(jnp.int32)
    return dict(queries=queries, keys=keys, values=values, out_grad=out_grad, block_position=block_position)


masked_value = -1.0e30


def reference(queries, keys, values, out_grad, block_position):
    root_scale = HD ** -0.5
    repeat = QH // KVH
    query_blocks = queries.reshape(BLOCKS, BLK, QH, HD)
    key_blocks = keys.reshape(BLOCKS, BLK, KVH, HD)
    value_blocks = values.reshape(BLOCKS, BLK, KVH, HD)
    grad_blocks = out_grad.reshape(BLOCKS, BLK, QH, HD)
    distance = jnp.arange(1, ROUNDS + 1, dtype=jnp.int32)
    causal = jnp.arange(BLK)[:, None] >= jnp.arange(BLK)[None, :]

    def one_block(carried, block_index):
        key_acc, value_acc = carried
        sources = jnp.concatenate([block_index[None], (block_index - distance) % BLOCKS]).astype(jnp.int32)
        key_set = jnp.tile(key_blocks[sources].reshape((ROUNDS + 1) * BLK, KVH, HD).astype(jnp.float32), (1, repeat, 1))
        value_set = jnp.tile(value_blocks[sources].reshape((ROUNDS + 1) * BLK, KVH, HD).astype(jnp.float32), (1, repeat, 1))
        earlier = block_position[sources[1:]] < block_position[block_index]
        far_mask = jnp.broadcast_to(jnp.repeat(earlier, BLK)[None, :], (BLK, ROUNDS * BLK))
        visible = jnp.concatenate([causal, far_mask], axis=1)
        query_set = query_blocks[block_index].astype(jnp.float32)
        grad_set = grad_blocks[block_index].astype(jnp.float32)
        scores = jnp.einsum("qhd,thd->hqt", query_set, key_set) * root_scale
        scores = jnp.where(visible[None], scores, masked_value)
        row_max = jnp.max(scores, axis=-1)
        row_sum = jnp.sum(jnp.exp(scores - row_max[..., None]), axis=-1)
        log_norm = row_max + jnp.log(row_sum)
        probs = jnp.exp(scores - log_norm[..., None])
        rounded = lax.optimization_barrier(probs.astype(jnp.bfloat16)).astype(jnp.float32)
        attended = jnp.einsum("hqt,thd->qhd", rounded, value_set).astype(jnp.bfloat16)
        row_dot = jnp.sum(grad_set * lax.optimization_barrier(attended).astype(jnp.float32), axis=-1).T
        grad_probs = jnp.einsum("qhd,thd->hqt", grad_set, value_set)
        grad_scores = lax.optimization_barrier((probs * (grad_probs - row_dot[..., None]) * root_scale).astype(jnp.bfloat16)).astype(jnp.float32)
        query_grad = jnp.einsum("hqt,thd->qhd", grad_scores, key_set).astype(jnp.bfloat16)
        key_grad = jnp.einsum("hqt,qhd->thd", grad_scores, query_set).reshape((ROUNDS + 1) * BLK, repeat, KVH, HD).sum(axis=1)
        value_grad = jnp.einsum("hqt,qhd->thd", rounded, grad_set).reshape((ROUNDS + 1) * BLK, repeat, KVH, HD).sum(axis=1)
        key_acc = key_acc.at[sources].add(key_grad.reshape(ROUNDS + 1, BLK, KVH, HD))
        value_acc = value_acc.at[sources].add(value_grad.reshape(ROUNDS + 1, BLK, KVH, HD))
        return (key_acc, value_acc), (attended, query_grad)

    start = (jnp.zeros((BLOCKS, BLK, KVH, HD), jnp.float32), jnp.zeros((BLOCKS, BLK, KVH, HD), jnp.float32))
    finals, stacked = lax.scan(one_block, start, jnp.arange(BLOCKS, dtype=jnp.int32))
    attended = stacked[0].reshape(TOKENS, QH * HD)
    query_grad = stacked[1].reshape(TOKENS, QH * HD)
    key_grad = finals[0].astype(jnp.bfloat16).reshape(TOKENS, KVH * HD)
    value_grad = finals[1].astype(jnp.bfloat16).reshape(TOKENS, KVH * HD)
    return (attended, query_grad, key_grad, value_grad)
```

```python
import functools

import jax
import jax.numpy as jnp
from jax import lax
from jax.experimental import pallas as pl
from jax.experimental.pallas import tpu as pltpu
from jax.sharding import PartitionSpec as P

KVH = 8
HD = 128
ROUNDS = 2
CHUNKS = 2
LOG2E = 1.4426950408889634
MASKED = -1e30


def dot(left, right, left_dim, right_dim):
    dims = (((left_dim,), (right_dim,)), ((), ()))
    return lax.dot_general(left, right, dims, preferred_element_type=jnp.float32)


def attend(place, order, q0, q1, d0, d1, key, value, far1, far2, a0, a1, g0, g1, near, back1, back2):
    rows = key.shape[0]
    scale = HD**-0.5
    query = jnp.concatenate([q0[...], q1[...]], 0)
    grad = jnp.concatenate([d0[...], d1[...]], 0)
    keys = [key[...], far1[:rows, :], far2[:rows, :]]
    values = [value[...], far1[rows:, :], far2[rows:, :]]
    own = order[place[0]]
    seen = [order[place[r]] < own for r in range(1, ROUNDS + 1)]
    scores = [dot(k, query, 1, 1) for k in keys]
    key_row = lax.broadcasted_iota(jnp.int32, (rows, 2 * rows), 0)
    query_row = lax.broadcasted_iota(jnp.int32, (rows, 2 * rows), 1) % rows
    scores[0] = jnp.where(key_row <= query_row, scores[0], MASKED)
    top = jnp.max(scores[0], 0, keepdims=True)
    for s, visible in zip(scores[1:], seen):
        top = jnp.maximum(top, jnp.where(visible, jnp.max(s, 0, keepdims=True), MASKED))
    tops = [top] + [jnp.where(visible, top, -MASKED) for visible in seen]
    probs = [jnp.exp2((s - t) * (scale * LOG2E)) for s, t in zip(scores, tops)]
    inverse = 1.0 / sum(jnp.sum(p, 0, keepdims=True) for p in probs)
    probs = [p * inverse for p in probs]
    rounded = [p.astype(jnp.bfloat16) for p in probs]
    out = sum(dot(v, p, 0, 0) for v, p in zip(values, rounded))
    attended = out.T.astype(jnp.bfloat16)
    a0[...] = attended[:rows]
    a1[...] = attended[rows:]
    row_dot = jnp.sum(
        grad.T.astype(jnp.float32) * out.astype(jnp.bfloat16).astype(jnp.float32), 0, keepdims=True
    )
    query_grad = 0.0
    for k, v, p, r, ref in zip(keys, values, probs, rounded, (near, back1, back2)):
        ds = (p * (dot(v, grad, 1, 1) - row_dot)).astype(jnp.bfloat16)
        ref[:rows, :] = (dot(ds, query, 1, 0) * scale).astype(ref.dtype)
        ref[rows:, :] = dot(r, grad, 1, 0).astype(ref.dtype)
        query_grad = query_grad + dot(k, ds, 0, 0)
    query_grad = (query_grad * scale).T.astype(jnp.bfloat16)
    g0[...] = query_grad[:rows]
    g1[...] = query_grad[rows:]


def head_of(chunk, t):
    half = KVH // CHUNKS // 2
    return (t // half) * (KVH // 2) + chunk * half + t % half


def attend_chunk(chunk, place, order, queries, out_grad, keys, values, far1, far2):
    rows = keys.shape[0]
    heads = KVH // CHUNKS
    width = heads * HD
    smem = pl.BlockSpec(memory_space=pltpu.SMEM)
    first = pl.BlockSpec((rows, HD), lambda t: (0, head_of(chunk, t)))
    second = pl.BlockSpec((rows, HD), lambda t: (0, head_of(chunk, t) + KVH))
    single = pl.BlockSpec((rows, HD), lambda t: (0, t))
    double = pl.BlockSpec((2 * rows, HD), lambda t: (0, t))
    flops = 6 * 2 * heads * (2 * rows) * (3 * rows) * HD
    return pl.pallas_call(
        attend,
        grid=(heads,),
        in_specs=[smem, smem, first, second, first, second, first, first, double, double],
        out_specs=[single] * 4 + [double] * 3,
        out_shape=[jax.ShapeDtypeStruct((rows, width), jnp.bfloat16)] * 4
        + [jax.ShapeDtypeStruct((2 * rows, width), jnp.float32)]
        + [jax.ShapeDtypeStruct((2 * rows, width), jnp.bfloat16)] * 2,
        compiler_params=pltpu.CompilerParams(vmem_limit_bytes=32 * 2**20),
        cost_estimate=pl.CostEstimate(
            flops=flops, bytes_accessed=12 * rows * width * 2, transcendentals=heads * 6 * rows * rows
        ),
    )(place, order, queries, queries, out_grad, out_grad, keys, values, far1, far2)


def columns(x, chunk):
    half = KVH // CHUNKS // 2 * HD
    middle = x.shape[1] // 2
    return jnp.concatenate(
        [x[:, chunk * half : (chunk + 1) * half], x[:, middle + chunk * half : middle + (chunk + 1) * half]], 1
    )


def on_device(queries, keys, values, out_grad, block_position):
    size = lax.axis_size("cp")
    position = lax.axis_index("cp")
    core = position % 2
    side = lax.axis_index("kv")
    place = (position - jnp.arange(ROUNDS + 1, dtype=jnp.int32)) % size
    ahead = [(i, (i + 2) % size) for i in range(size)]
    behind = [((i + 2) % size, i) for i in range(size)]
    swap = [(i, i ^ 1) for i in range(size)]
    across = [(0, 1), (1, 0)]
    bf16, f32 = jnp.bfloat16, jnp.float32
    rows = keys.shape[0]

    own = [jnp.concatenate([columns(keys, c), columns(values, c)], 0) for c in range(CHUNKS)]
    far2, far1 = [], []
    for c in range(CHUNKS):
        x = own[c]
        if c:
            x, _ = lax.optimization_barrier((x, far2[-1]))
        far2.append(lax.ppermute(x, "cp", ahead))
    for c in range(CHUNKS):
        far1.append(lax.ppermute(jnp.where(core == 0, own[c], far2[c]), "cp", swap))
    parts = []
    total = []
    for c in range(CHUNKS):
        a0, a1, g0, g1, near, back1, back2 = attend_chunk(
            c, place, block_position, queries, out_grad, keys, values, far1[c], far2[c]
        )
        parts.append((a0, a1, g0, g1))
        got = lax.ppermute(back1, "cp", swap)
        zero = jnp.zeros((), f32)
        got = got.astype(f32)
        summed = (back2.astype(f32) + jnp.where(core == 1, got, zero)).astype(bf16)
        arrived = lax.ppermute(summed, "cp", behind)
        mine = near + jnp.where(core == 0, got, zero) + arrived.astype(f32)
        half = mine.shape[1] // 2
        give = jnp.where(side == 0, mine[:, half:], mine[:, :half]).astype(bf16)
        keep = jnp.where(side == 0, mine[:, :half], mine[:, half:])
        total.append((keep + lax.ppermute(give, "kv", across).astype(f32)).astype(bf16))

    def join(index):
        halves = KVH // CHUNKS // 2 * HD
        pieces = []
        for g in (0, 1):
            for h in (0, 1):
                pieces += [p[index + g][:, h * halves : (h + 1) * halves] for p in parts]
        return jnp.concatenate(pieces, 1)

    key_grad = jnp.concatenate([t[:rows] for t in total], 1)
    value_grad = jnp.concatenate([t[rows:] for t in total], 1)
    return join(0), join(2), key_grad, value_grad


def solution(mesh):
    placed = (P("cp", "kv"), P("cp", None), P("cp", None), P("cp", "kv"), P())
    return jax.shard_map(
        on_device,
        mesh=mesh,
        in_specs=placed,
        out_specs=(P("cp", "kv"), P("cp", "kv"), P("cp", "kv"), P("cp", "kv")),
        check_vma=False,
    )
```

```python
import jax
import jax.numpy as jnp
from jax import lax
from jax.experimental import pallas as pl
from jax.experimental.pallas import tpu as pltpu
from jax.sharding import PartitionSpec as P

KVH = 8
HD = 128
ROUNDS = 2
UNITS = 4
LOG2E = 1.4426950408889634
MASKED = -1e30
VMEM_LIMIT = 20 * 2**20


def dot(left, right, left_dim, right_dim):
    dims = (((left_dim,), (right_dim,)), ((), ()))
    return lax.dot_general(left, right, dims, preferred_element_type=jnp.float32)


def pack(place, *refs):
    ins, outs = refs[: 2 * UNITS], refs[2 * UNITS :]
    rows = ins[0].shape[0]
    for u, out in enumerate(outs):
        out[:rows, :] = ins[2 * u][...]
        out[rows:, :] = ins[2 * u + 1][...]


def finish(near0, near1, crossed, arrived0, arrived1, key_grad, value_grad):
    rows, width = key_grad.shape[0], near0.shape[1]
    for u, (near, arrived) in enumerate(((near0, arrived0), (near1, arrived1))):
        total = near[...] + crossed[u].astype(jnp.float32) + arrived[...].astype(jnp.float32)
        total = total.astype(jnp.bfloat16)
        key_grad[:, u * width : (u + 1) * width] = total[:rows]
        value_grad[:, u * width : (u + 1) * width] = total[rows:]


def attend(place, order, q0, q1, d0, d1, key, value, near_key, near_value, far1, far2, *outs):
    a0, a1, g0, g1, near, back1, back2 = outs
    rows = key.shape[0]
    scale = HD**-0.5
    position, size = place[0], order.shape[0]
    seen = [order[(position + size - r) % size] < order[position] for r in range(1, ROUNDS + 1)]
    first_core = position % 2 == 0
    key_row = lax.broadcasted_iota(jnp.int32, (rows, 2 * rows), 0)
    query_row = lax.broadcasted_iota(jnp.int32, (rows, 2 * rows), 1) % rows
    causal = key_row <= query_row
    for head in range(key.shape[1] // HD):
        c = slice(head * HD, (head + 1) * HD)
        query = jnp.concatenate([q0[:, c], q1[:, c]], 0)
        grad = jnp.concatenate([d0[:, c], d1[:, c]], 0)
        keys = [key[:, c], jnp.where(first_core, far1[:rows, c], near_key[:, c]), far2[:rows, c]]
        values = [value[:, c], jnp.where(first_core, far1[rows:, c], near_value[:, c]), far2[rows:, c]]
        scores = [dot(k, query, 1, 1) for k in keys]
        scores[0] = jnp.where(causal, scores[0], MASKED)
        top = jnp.max(scores[0], 0, keepdims=True)
        for s, visible in zip(scores[1:], seen):
            top = jnp.maximum(top, jnp.where(visible, jnp.max(s, 0, keepdims=True), MASKED))
        tops = [top] + [jnp.where(visible, top, -MASKED) for visible in seen]
        probs = [jnp.exp2((s - t) * (scale * LOG2E)) for s, t in zip(scores, tops)]
        inverse = 1.0 / sum(jnp.sum(p, 0, keepdims=True) for p in probs)
        probs = [p.astype(jnp.bfloat16) for p in probs]
        out = sum(dot(v, p, 0, 0) for v, p in zip(values, probs)) * inverse
        attended = out.T.astype(jnp.bfloat16)
        a0[:, c] = attended[:rows]
        a1[:, c] = attended[rows:]
        scaled = (grad.T.astype(jnp.float32) * inverse).astype(jnp.bfloat16)
        scaled_rows = scaled.T
        row_dot = jnp.sum(scaled.astype(jnp.float32) * out, 0, keepdims=True)
        query_grad = 0.0
        for k, v, p, ref in zip(keys, values, probs, (near, back1, back2)):
            ds = p * (dot(v, scaled, 1, 0) - row_dot).astype(jnp.bfloat16)
            ref[:rows, c] = (dot(ds, query, 1, 0) * scale).astype(ref.dtype)
            ref[rows:, c] = dot(p, scaled_rows, 1, 0).astype(ref.dtype)
            query_grad = query_grad + dot(k, ds, 0, 0)
        query_grad = (query_grad * scale).T.astype(jnp.bfloat16)
        g0[:, c] = query_grad[:rows]
        g1[:, c] = query_grad[rows:]


def unit_at(u, place):
    side = place[1]
    return jnp.where(u < UNITS // 2, 1 - side, side) * (UNITS // 2) + u % (UNITS // 2)


def pack_units(place, keys, values):
    rows, width = keys.shape[0], keys.shape[1] // UNITS
    specs = []
    for u in range(UNITS):
        specs += [pl.BlockSpec((rows, width), lambda t, place, u=u: (0, unit_at(u, place)))] * 2
    return pl.pallas_call(
        pack,
        grid_spec=pltpu.PrefetchScalarGridSpec(
            num_scalar_prefetch=1,
            grid=(1,),
            in_specs=specs,
            out_specs=[pl.BlockSpec((2 * rows, width), lambda t, place: (0, 0))] * UNITS,
        ),
        out_shape=[jax.ShapeDtypeStruct((2 * rows, width), keys.dtype)] * UNITS,
        compiler_params=pltpu.CompilerParams(vmem_limit_bytes=VMEM_LIMIT),
        cost_estimate=pl.CostEstimate(flops=0, bytes_accessed=8 * keys.size, transcendentals=0),
    )(place, *([keys, values] * UNITS))


def attend_unit(u, place, order, queries, out_grad, keys, values, near_keys, near_values, far1, far2):
    rows = keys.shape[0]
    width = far1.shape[1]
    heads = width // HD
    first = pl.BlockSpec((rows, width), lambda t, place, order: (0, unit_at(u, place)))
    second = pl.BlockSpec((rows, width), lambda t, place, order: (0, unit_at(u, place) + UNITS))
    single = pl.BlockSpec((rows, width), lambda t, place, order: (0, 0))
    double = pl.BlockSpec((2 * rows, width), lambda t, place, order: (0, 0))
    return pl.pallas_call(
        attend,
        grid_spec=pltpu.PrefetchScalarGridSpec(
            num_scalar_prefetch=2,
            grid=(1,),
            in_specs=[first, second, first, second, first, first, first, first, double, double],
            out_specs=[single] * 4 + [double] * 3,
        ),
        out_shape=[jax.ShapeDtypeStruct((rows, width), jnp.bfloat16)] * 4
        + [jax.ShapeDtypeStruct((2 * rows, width), jnp.float32)]
        + [jax.ShapeDtypeStruct((2 * rows, width), jnp.bfloat16)] * 2,
        compiler_params=pltpu.CompilerParams(vmem_limit_bytes=VMEM_LIMIT),
        cost_estimate=pl.CostEstimate(
            flops=6 * 2 * heads * (2 * rows) * (3 * rows) * HD,
            bytes_accessed=12 * rows * width * 2,
            transcendentals=heads * 6 * rows * rows,
        ),
    )(place, order, queries, queries, out_grad, out_grad, keys, values, near_keys, near_values, far1, far2)


def on_device(queries, keys, values, out_grad, block_position):
    size = lax.axis_size("cp")
    position = lax.axis_index("cp")
    core = position % 2
    side = lax.axis_index("kv")
    ahead = [(i, (i + 2) % size) for i in range(size)]
    behind = [((i + 2) % size, i) for i in range(size)]
    swap = [(i, i ^ 1) for i in range(size)]
    across = [(0, 1), (1, 0)]
    bf16, f32 = jnp.bfloat16, jnp.float32
    rows = keys.shape[0]
    zero = jnp.zeros((), f32)
    place = jnp.stack([position, side]).astype(jnp.int32)
    keys, values, queries, out_grad = [
        pltpu.with_memory_space_constraint(x, pltpu.HBM) for x in (keys, values, queries, out_grad)
    ]

    own = pack_units(place, keys, values)
    far2 = [lax.ppermute(x, "cp", ahead) for x in own]
    near_keys = lax.ppermute(keys, "cp", swap)
    near_values = lax.ppermute(values, "cp", swap)
    results, near, arrived = [], [], []
    crossed = []
    send = None
    for u in range(UNITS):
        if u:
            far2[u], _ = lax.optimization_barrier((far2[u], back1))
        far1 = lax.ppermute(far2[u], "cp", swap)
        if u:
            far1, _ = lax.optimization_barrier((far1, send))
        *outs, part, back1, back2 = attend_unit(
            u, place, block_position, queries, out_grad, keys, values, near_keys, near_values, far1, far2[u]
        )
        results.append(outs)
        got = lax.ppermute(back1, "cp", swap).astype(f32)
        near.append(part + jnp.where(core == 0, got, zero))
        send = back2.astype(f32) + jnp.where(core == 1, got, zero)
        if u < UNITS // 2:
            send = send.astype(bf16)
            crossed.append(lax.ppermute(send, "kv", across))
        else:
            send = (send + crossed[u - UNITS // 2].astype(f32)).astype(bf16)
            arrived.append(lax.ppermute(send, "cp", behind))
    near_crossed = lax.ppermute(jnp.stack([near[0], near[1]]).astype(bf16), "kv", across)
    key_grad, value_grad = pl.pallas_call(
        finish,
        out_shape=[jax.ShapeDtypeStruct((rows, keys.shape[1] // 2), bf16)] * 2,
        compiler_params=pltpu.CompilerParams(vmem_limit_bytes=VMEM_LIMIT),
    )(near[2], near[3], near_crossed, *arrived)

    def join(index):
        pieces = []
        for g in (0, 1):
            other = jnp.concatenate([results[0][index + g], results[1][index + g]], 1)
            mine = jnp.concatenate([results[2][index + g], results[3][index + g]], 1)
            pieces += [jnp.where(side == 0, mine, other), jnp.where(side == 0, other, mine)]
        return jnp.concatenate(pieces, 1)

    return join(0), join(2), key_grad, value_grad


def solution(mesh):
    placed = (P("cp", "kv"), P("cp", None), P("cp", None), P("cp", "kv"), P())
    return jax.shard_map(
        on_device,
        mesh=mesh,
        in_specs=placed,
        out_specs=(P("cp", "kv"), P("cp", "kv"), P("cp", "kv"), P("cp", "kv")),
        check_vma=False,
    )
```

```python
import jax
import jax.numpy as jnp
from jax import lax
from jax.experimental import pallas as pl
from jax.experimental.pallas import tpu as pltpu
from jax.sharding import PartitionSpec as P

KVH = 8
HD = 128
ROUNDS = 2
UNITS = 4
LOG2E = 1.4426950408889634
MASKED = -1e30
VMEM_LIMIT = 20 * 2**20


def dot(left, right, left_dim, right_dim):
    dims = (((left_dim,), (right_dim,)), ((), ()))
    return lax.dot_general(left, right, dims, preferred_element_type=jnp.float32)


def pack(place, *refs):
    ins, outs = refs[: 2 * UNITS], refs[2 * UNITS :]
    rows = ins[0].shape[0]
    for u, out in enumerate(outs):
        out[:rows, :] = ins[2 * u][...]
        out[rows:, :] = ins[2 * u + 1][...]


def stage(place, *refs):
    ins, outs = refs[: 8 * UNITS], refs[8 * UNITS :]
    rows, width = ins[0].shape
    for u, out in enumerate(outs):
        for n in range(8):
            at = slice(n // 2 * width, (n // 2 + 1) * width)
            out[n % 2 * rows : (n % 2 + 1) * rows, at] = ins[8 * u + n][...]


def finish(near0, near1, crossed, arrived0, arrived1, key_grad, value_grad):
    rows, width = key_grad.shape[0], near0.shape[1]
    for u, (near, arrived) in enumerate(((near0, arrived0), (near1, arrived1))):
        total = near[...] + crossed[u].astype(jnp.float32) + arrived[...].astype(jnp.float32)
        total = total.astype(jnp.bfloat16)
        key_grad[:, u * width : (u + 1) * width] = total[:rows]
        value_grad[:, u * width : (u + 1) * width] = total[rows:]


def attend(place, order, heads, far1, far2, *outs):
    a0, a1, g0, g1, near, back1, back2 = outs
    rows, width = far1.shape[0] // 2, far1.shape[1]
    scale = HD**-0.5
    position, size = place[0], order.shape[0]
    seen = [order[(position + size - r) % size] < order[position] for r in range(1, ROUNDS + 1)]
    first_core = position % 2 == 0
    key_row = lax.broadcasted_iota(jnp.int32, (rows, 2 * rows), 0)
    query_row = lax.broadcasted_iota(jnp.int32, (rows, 2 * rows), 1) % rows
    causal = key_row <= query_row
    for head in range(width // HD):
        c = slice(head * HD, (head + 1) * HD)
        query, grad, own, beside = [heads[:, n * width + head * HD : n * width + (head + 1) * HD] for n in range(4)]
        keys = [own[:rows], jnp.where(first_core, far1[:rows, c], beside[:rows]), far2[:rows, c]]
        values = [own[rows:], jnp.where(first_core, far1[rows:, c], beside[rows:]), far2[rows:, c]]
        scores = [dot(k, query, 1, 1) for k in keys]
        scores[0] = jnp.where(causal, scores[0], MASKED)
        top = jnp.max(scores[0], 0, keepdims=True)
        for s, visible in zip(scores[1:], seen):
            top = jnp.maximum(top, jnp.where(visible, jnp.max(s, 0, keepdims=True), MASKED))
        tops = [top] + [jnp.where(visible, top, -MASKED) for visible in seen]
        probs = [jnp.exp2((s - t) * (scale * LOG2E)) for s, t in zip(scores, tops)]
        inverse = 1.0 / sum(jnp.sum(p, 0, keepdims=True) for p in probs)
        probs = [p.astype(jnp.bfloat16) for p in probs]
        out = sum(dot(v, p, 0, 0) for v, p in zip(values, probs)) * inverse
        attended = out.T.astype(jnp.bfloat16)
        a0[:, c] = attended[:rows]
        a1[:, c] = attended[rows:]
        scaled = (grad.T.astype(jnp.float32) * inverse).astype(jnp.bfloat16)
        scaled_rows = scaled.T
        row_dot = jnp.sum(scaled.astype(jnp.float32) * out, 0, keepdims=True)
        query_grad = 0.0
        for k, v, p, ref in zip(keys, values, probs, (near, back1, back2)):
            ds = p * (dot(v, scaled, 1, 0) - row_dot).astype(jnp.bfloat16)
            ref[:rows, c] = (dot(ds, query, 1, 0) * scale).astype(ref.dtype)
            ref[rows:, c] = dot(p, scaled_rows, 1, 0).astype(ref.dtype)
            query_grad = query_grad + dot(k, ds, 0, 0)
        query_grad = (query_grad * scale).T.astype(jnp.bfloat16)
        g0[:, c] = query_grad[:rows]
        g1[:, c] = query_grad[rows:]


def unit_at(u, place):
    side = place[1]
    return jnp.where(u < UNITS // 2, 1 - side, side) * (UNITS // 2) + u % (UNITS // 2)


def pack_units(place, keys, values):
    rows, width = keys.shape[0], keys.shape[1] // UNITS
    specs = []
    for u in range(UNITS):
        specs += [pl.BlockSpec((rows, width), lambda t, place, u=u: (0, unit_at(u, place)))] * 2
    return pl.pallas_call(
        pack,
        grid_spec=pltpu.PrefetchScalarGridSpec(
            num_scalar_prefetch=1,
            grid=(1,),
            in_specs=specs,
            out_specs=[pl.BlockSpec((2 * rows, width), lambda t, place: (0, 0))] * UNITS,
        ),
        out_shape=[jax.ShapeDtypeStruct((2 * rows, width), keys.dtype)] * UNITS,
        compiler_params=pltpu.CompilerParams(vmem_limit_bytes=VMEM_LIMIT),
        cost_estimate=pl.CostEstimate(flops=0, bytes_accessed=8 * keys.size, transcendentals=0),
    )(place, *([keys, values] * UNITS))


def stage_heads(place, queries, out_grad, keys, values, near_keys, near_values, width):
    rows = queries.shape[0]
    specs = [
        pl.BlockSpec((rows, width), lambda t, place, u=u, g=g: (0, unit_at(u, place) + g * UNITS))
        for u in range(UNITS)
        for g in (0, 1, 0, 1, 0, 0, 0, 0)
    ]
    shape = (2 * rows, 4 * width)
    return pl.pallas_call(
        stage,
        grid_spec=pltpu.PrefetchScalarGridSpec(
            num_scalar_prefetch=1,
            grid=(1,),
            in_specs=specs,
            out_specs=[pl.BlockSpec(shape, lambda t, place: (0, 0))] * UNITS,
        ),
        out_shape=[jax.ShapeDtypeStruct(shape, queries.dtype)] + [pltpu.HBM(shape, queries.dtype)] * (UNITS - 1),
        compiler_params=pltpu.CompilerParams(vmem_limit_bytes=VMEM_LIMIT),
    )(place, *([queries, queries, out_grad, out_grad, keys, values, near_keys, near_values] * UNITS))


def attend_unit(u, place, order, heads, far1, far2):
    rows = far1.shape[0] // 2
    width = far1.shape[1]
    staged = pl.BlockSpec((2 * rows, 4 * width), lambda t, place, order: (0, 0))
    single = pl.BlockSpec((rows, width), lambda t, place, order: (0, 0))
    double = pl.BlockSpec((2 * rows, width), lambda t, place, order: (0, 0))
    return pl.pallas_call(
        attend,
        grid_spec=pltpu.PrefetchScalarGridSpec(
            num_scalar_prefetch=2,
            grid=(1,),
            in_specs=[staged, double, double],
            out_specs=[single] * 4 + [double] * 3,
        ),
        out_shape=[jax.ShapeDtypeStruct((rows, width), jnp.bfloat16)] * 4
        + [jax.ShapeDtypeStruct((2 * rows, width), jnp.bfloat16)] * 3,
        compiler_params=pltpu.CompilerParams(vmem_limit_bytes=VMEM_LIMIT),
    )(place, order, heads, far1, far2)


def on_device(queries, keys, values, out_grad, block_position):
    size = lax.axis_size("cp")
    position = lax.axis_index("cp")
    core = position % 2
    side = lax.axis_index("kv")
    ahead = [(i, (i + 2) % size) for i in range(size)]
    behind = [((i + 2) % size, i) for i in range(size)]
    swap = [(i, i ^ 1) for i in range(size)]
    across = [(0, 1), (1, 0)]
    bf16, f32 = jnp.bfloat16, jnp.float32
    rows = keys.shape[0]
    zero = jnp.zeros((), f32)
    place = jnp.stack([position, side]).astype(jnp.int32)
    raw_keys, raw_values = keys, values
    keys, values, queries, out_grad = [
        pltpu.with_memory_space_constraint(x, pltpu.HBM) for x in (keys, values, queries, out_grad)
    ]

    own = pack_units(place, keys, values)
    far2 = [lax.ppermute(x, "cp", ahead) for x in own]
    raw_keys, raw_values, _ = lax.optimization_barrier((raw_keys, raw_values, own[0]))
    near_keys = lax.ppermute(raw_keys, "cp", swap)
    near_values = lax.ppermute(raw_values, "cp", swap)
    heads = stage_heads(
        place, queries, out_grad, keys, values, near_keys, near_values, own[0].shape[1]
    )
    far2[0], _ = lax.optimization_barrier((far2[0], heads[0]))
    results, near, arrived = [], [], []
    crossed = []
    send = None
    for u in range(UNITS):
        if u:
            far2[u], _ = lax.optimization_barrier((far2[u], back1))
        far1 = lax.ppermute(far2[u], "cp", swap)
        if u:
            far1, _ = lax.optimization_barrier((far1, send))
        *outs, part, back1, back2 = attend_unit(
            u, place, block_position, heads[u], far1, far2[u]
        )
        results.append(outs)
        got = lax.ppermute(back1, "cp", swap).astype(f32)
        near.append(part + jnp.where(core == 0, got, zero))
        send = back2.astype(f32) + jnp.where(core == 1, got, zero)
        if u < UNITS // 2:
            send = send.astype(bf16)
            crossed.append(lax.ppermute(send, "kv", across))
        else:
            send = (send + crossed[u - UNITS // 2].astype(f32)).astype(bf16)
            arrived.append(lax.ppermute(send, "cp", behind))
    near_crossed = lax.ppermute(jnp.stack([near[0], near[1]]).astype(bf16), "kv", across)
    key_grad, value_grad = pl.pallas_call(
        finish,
        out_shape=[jax.ShapeDtypeStruct((rows, keys.shape[1] // 2), bf16)] * 2,
        compiler_params=pltpu.CompilerParams(vmem_limit_bytes=VMEM_LIMIT),
    )(near[2], near[3], near_crossed, *arrived)

    def join(index):
        pieces = []
        for g in (0, 1):
            other = jnp.concatenate([results[0][index + g], results[1][index + g]], 1)
            mine = jnp.concatenate([results[2][index + g], results[3][index + g]], 1)
            pieces += [jnp.where(side == 0, mine, other), jnp.where(side == 0, other, mine)]
        return jnp.concatenate(pieces, 1)

    return join(0), join(2), key_grad, value_grad


def solution(mesh):
    placed = (P("cp", "kv"), P("cp", None), P("cp", None), P("cp", "kv"), P())
    return jax.shard_map(
        on_device,
        mesh=mesh,
        in_specs=placed,
        out_specs=(P("cp", "kv"), P("cp", "kv"), P("cp", "kv"), P("cp", "kv")),
        check_vma=False,
    )
```

```python
import jax
import jax.numpy as jnp
from jax import lax
from jax.experimental import pallas as pl
from jax.experimental.pallas import tpu as pltpu
from jax.sharding import PartitionSpec as P

KVH = 8
HD = 128
ROUNDS = 2
UNITS = 4
LOG2E = 1.4426950408889634
MASKED = -1e30
VMEM_LIMIT = 20 * 2**20


def dot(left, right, left_dim, right_dim):
    dims = (((left_dim,), (right_dim,)), ((), ()))
    return lax.dot_general(left, right, dims, preferred_element_type=jnp.float32)


def pack(place, *refs):
    ins, outs = refs[:2], refs[2:]
    rows = ins[0].shape[0]
    for u, out in enumerate(outs):
        out[:rows, :] = ins[2 * u][...]
        out[rows:, :] = ins[2 * u + 1][...]


def stage(place, *refs):
    ins, outs, packed = refs[: 8 * UNITS], refs[8 * UNITS : 9 * UNITS], refs[9 * UNITS :]
    rows, width = ins[0].shape
    for u, out in enumerate(outs):
        for n in range(8):
            at = slice(n // 2 * width, (n // 2 + 1) * width)
            out[n % 2 * rows : (n % 2 + 1) * rows, at] = ins[8 * u + n][...]
        if u:
            packed[u - 1][:rows, :] = ins[8 * u + 4][...]
            packed[u - 1][rows:, :] = ins[8 * u + 5][...]


def finish(near0, near1, crossed, arrived0, arrived1, key_grad, value_grad):
    rows, width = key_grad.shape[0], near0.shape[1]
    for u, (near, arrived) in enumerate(((near0, arrived0), (near1, arrived1))):
        total = near[...] + crossed[u].astype(jnp.float32) + arrived[...].astype(jnp.float32)
        total = total.astype(jnp.bfloat16)
        key_grad[:, u * width : (u + 1) * width] = total[:rows]
        value_grad[:, u * width : (u + 1) * width] = total[rows:]


def attend(place, order, heads, far1, far2, *outs):
    a0, a1, g0, g1, near, back1, back2 = outs
    rows, width = far1.shape[0] // 2, far1.shape[1]
    scale = HD**-0.5
    position, size = place[0], order.shape[0]
    seen = [order[(position + size - r) % size] < order[position] for r in range(1, ROUNDS + 1)]
    first_core = position % 2 == 0
    key_row = lax.broadcasted_iota(jnp.int32, (rows, 2 * rows), 0)
    query_row = lax.broadcasted_iota(jnp.int32, (rows, 2 * rows), 1) % rows
    causal = key_row <= query_row
    for head in range(width // HD):
        c = slice(head * HD, (head + 1) * HD)
        query, grad, own, beside = [heads[:, n * width + head * HD : n * width + (head + 1) * HD] for n in range(4)]
        keys = [own[:rows], jnp.where(first_core, far1[:rows, c], beside[:rows]), far2[:rows, c]]
        values = [own[rows:], jnp.where(first_core, far1[rows:, c], beside[rows:]), far2[rows:, c]]
        scores = [dot(k, query, 1, 1) for k in keys]
        scores[0] = jnp.where(causal, scores[0], MASKED)
        top = jnp.max(scores[0], 0, keepdims=True)
        for s, visible in zip(scores[1:], seen):
            top = jnp.maximum(top, jnp.where(visible, jnp.max(s, 0, keepdims=True), MASKED))
        tops = [top] + [jnp.where(visible, top, -MASKED) for visible in seen]
        probs = [jnp.exp2((s - t) * (scale * LOG2E)) for s, t in zip(scores, tops)]
        inverse = 1.0 / sum(jnp.sum(p, 0, keepdims=True) for p in probs)
        probs = [p.astype(jnp.bfloat16) for p in probs]
        out = sum(dot(v, p, 0, 0) for v, p in zip(values, probs)) * inverse
        attended = out.T.astype(jnp.bfloat16)
        a0[:, c] = attended[:rows]
        a1[:, c] = attended[rows:]
        scaled = (grad.T.astype(jnp.float32) * inverse).astype(jnp.bfloat16)
        scaled_rows = scaled.T
        row_dot = jnp.sum(scaled.astype(jnp.float32) * out, 0, keepdims=True)
        query_grad = 0.0
        for k, v, p, ref in zip(keys, values, probs, (near, back1, back2)):
            ds = p * (dot(v, scaled, 1, 0) - row_dot).astype(jnp.bfloat16)
            ref[:rows, c] = (dot(ds, query, 1, 0) * scale).astype(ref.dtype)
            ref[rows:, c] = dot(p, scaled_rows, 1, 0).astype(ref.dtype)
            query_grad = query_grad + dot(k, ds, 0, 0)
        query_grad = (query_grad * scale).T.astype(jnp.bfloat16)
        g0[:, c] = query_grad[:rows]
        g1[:, c] = query_grad[rows:]


def unit_at(u, place):
    side = place[1]
    return jnp.where(u < UNITS // 2, 1 - side, side) * (UNITS // 2) + u % (UNITS // 2)


def pack_units(place, keys, values):
    rows, width = keys.shape[0], keys.shape[1] // UNITS
    specs = []
    for u in range(1):
        specs += [pl.BlockSpec((rows, width), lambda t, place, u=u: (0, unit_at(u, place)))] * 2
    return pl.pallas_call(
        pack,
        grid_spec=pltpu.PrefetchScalarGridSpec(
            num_scalar_prefetch=1,
            grid=(1,),
            in_specs=specs,
            out_specs=[pl.BlockSpec((2 * rows, width), lambda t, place: (0, 0))] * 1,
        ),
        out_shape=[jax.ShapeDtypeStruct((2 * rows, width), keys.dtype)] * 1,
        compiler_params=pltpu.CompilerParams(vmem_limit_bytes=VMEM_LIMIT),
        cost_estimate=pl.CostEstimate(flops=0, bytes_accessed=8 * keys.size, transcendentals=0),
    )(place, keys, values)


def stage_heads(place, queries, out_grad, keys, values, near_keys, near_values, width):
    rows = queries.shape[0]
    specs = [
        pl.BlockSpec((rows, width), lambda t, place, u=u, g=g: (0, unit_at(u, place) + g * UNITS))
        for u in range(UNITS)
        for g in (0, 1, 0, 1, 0, 0, 0, 0)
    ]
    shape = (2 * rows, 4 * width)
    return pl.pallas_call(
        stage,
        grid_spec=pltpu.PrefetchScalarGridSpec(
            num_scalar_prefetch=1,
            grid=(1,),
            in_specs=specs,
            out_specs=[pl.BlockSpec(shape, lambda t, place: (0, 0))] * UNITS
            + [pl.BlockSpec((2 * rows, width), lambda t, place: (0, 0))] * (UNITS - 1),
        ),
        out_shape=[jax.ShapeDtypeStruct(shape, queries.dtype)] + [pltpu.HBM(shape, queries.dtype)] * (UNITS - 1)
        + [jax.ShapeDtypeStruct((2 * rows, width), keys.dtype)] * (UNITS - 1),
        compiler_params=pltpu.CompilerParams(vmem_limit_bytes=VMEM_LIMIT),
    )(place, *([queries, queries, out_grad, out_grad, keys, values, near_keys, near_values] * UNITS))


def attend_unit(u, place, order, heads, far1, far2):
    rows = far1.shape[0] // 2
    width = far1.shape[1]
    staged = pl.BlockSpec((2 * rows, 4 * width), lambda t, place, order: (0, 0))
    single = pl.BlockSpec((rows, width), lambda t, place, order: (0, 0))
    double = pl.BlockSpec((2 * rows, width), lambda t, place, order: (0, 0))
    return pl.pallas_call(
        attend,
        grid_spec=pltpu.PrefetchScalarGridSpec(
            num_scalar_prefetch=2,
            grid=(1,),
            in_specs=[staged, double, double],
            out_specs=[single] * 4 + [double] * 3,
        ),
        out_shape=[jax.ShapeDtypeStruct((rows, width), jnp.bfloat16)] * 4
        + [jax.ShapeDtypeStruct((2 * rows, width), jnp.bfloat16)] * 3,
        compiler_params=pltpu.CompilerParams(vmem_limit_bytes=VMEM_LIMIT),
    )(place, order, heads, far1, far2)


def on_device(queries, keys, values, out_grad, block_position):
    size = lax.axis_size("cp")
    position = lax.axis_index("cp")
    core = position % 2
    side = lax.axis_index("kv")
    ahead = [(i, (i + 2) % size) for i in range(size)]
    behind = [((i + 2) % size, i) for i in range(size)]
    swap = [(i, i ^ 1) for i in range(size)]
    across = [(0, 1), (1, 0)]
    bf16, f32 = jnp.bfloat16, jnp.float32
    rows = keys.shape[0]
    zero = jnp.zeros((), f32)
    place = jnp.stack([position, side]).astype(jnp.int32)
    raw_keys, raw_values = keys, values
    keys, values, queries, out_grad = [
        pltpu.with_memory_space_constraint(x, pltpu.HBM) for x in (keys, values, queries, out_grad)
    ]

    own = pack_units(place, keys, values)
    far2 = [lax.ppermute(own[0], "cp", ahead)]
    raw_keys, raw_values, _ = lax.optimization_barrier((raw_keys, raw_values, own[0]))
    near_keys = lax.ppermute(raw_keys, "cp", swap)
    near_values = lax.ppermute(raw_values, "cp", swap)
    staged = stage_heads(
        place, queries, out_grad, keys, values, near_keys, near_values, own[0].shape[1]
    )
    heads = staged[:UNITS]
    far2 += [lax.ppermute(x, "cp", ahead) for x in staged[UNITS:]]
    far2[0], _ = lax.optimization_barrier((far2[0], heads[0]))
    results, near, arrived = [], [], []
    crossed = []
    send = None
    for u in range(UNITS):
        if u:
            far2[u], _ = lax.optimization_barrier((far2[u], back1))
        far1 = lax.ppermute(far2[u], "cp", swap)
        if u:
            far1, _ = lax.optimization_barrier((far1, send))
        *outs, part, back1, back2 = attend_unit(
            u, place, block_position, heads[u], far1, far2[u]
        )
        results.append(outs)
        got = lax.ppermute(back1, "cp", swap).astype(f32)
        near.append(part + jnp.where(core == 0, got, zero))
        send = back2.astype(f32) + jnp.where(core == 1, got, zero)
        if u < UNITS // 2:
            send = send.astype(bf16)
            crossed.append(lax.ppermute(send, "kv", across))
        else:
            send = (send + crossed[u - UNITS // 2].astype(f32)).astype(bf16)
            arrived.append(lax.ppermute(send, "cp", behind))
    near_crossed = lax.ppermute(jnp.stack([near[0], near[1]]).astype(bf16), "kv", across)
    key_grad, value_grad = pl.pallas_call(
        finish,
        out_shape=[jax.ShapeDtypeStruct((rows, keys.shape[1] // 2), bf16)] * 2,
        compiler_params=pltpu.CompilerParams(vmem_limit_bytes=VMEM_LIMIT),
    )(near[2], near[3], near_crossed, *arrived)

    def join(index):
        pieces = []
        for g in (0, 1):
            other = jnp.concatenate([results[0][index + g], results[1][index + g]], 1)
            mine = jnp.concatenate([results[2][index + g], results[3][index + g]], 1)
            pieces += [jnp.where(side == 0, mine, other), jnp.where(side == 0, other, mine)]
        return jnp.concatenate(pieces, 1)

    return join(0), join(2), key_grad, value_grad


def solution(mesh):
    placed = (P("cp", "kv"), P("cp", None), P("cp", None), P("cp", "kv"), P())
    return jax.shard_map(
        on_device,
        mesh=mesh,
        in_specs=placed,
        out_specs=(P("cp", "kv"), P("cp", "kv"), P("cp", "kv"), P("cp", "kv")),
        check_vma=False,
    )
```
